32 devices in a mesh: gy: 4 (over y, core), gz: 8 (over z, x).
Axes of the slice: x: 2, y: 2, z: 4, core: 2. Of those that a mesh axis runs over, the one named last changes fastest.
Arguments:
- offset: float32 [3, 65536], P(None, ('gy', 'gz')), may hold values from 0.6 to 1.4
- velocity: float32 [3, 65536], P(None, ('gy', 'gz')), may hold values from -4 to 4
- affine: float32 [9, 65536], P(None, ('gy', 'gz')), may hold values from -3 to 3
- deform: float32 [9, 65536], P(None, ('gy', 'gz')), as said below
- cell_index: int32 [65536], P(('gy', 'gz')), may hold values from 1 to 16382, as said below
- live_count: int32 [32], P(('gy', 'gz')), may hold values from 128 to 2048, as said below
- grip_mask: int32 [64, 64, 128], P('gy', 'gz'), may hold values from 0 to 2
- grip_velocity: float32 [2, 2, 3], replicated, may hold values from -4 to 4
- loss_offset: float32 [3, 65536], P(None, ('gy', 'gz')), may hold values from -6 to 6
- loss_velocity: float32 [3, 65536], P(None, ('gy', 'gz')), may hold values from -6 to 6
- loss_affine: float32 [9, 65536], P(None, ('gy', 'gz')), may hold values from -6 to 6
- loss_deform: float32 [9, 65536], P(None, ('gy', 'gz')), may hold values from -6 to 6
Outputs:
- grad_offset: float32 [3, 65536], P(None, ('gy', 'gz'))
- grad_velocity: float32 [3, 65536], P(None, ('gy', 'gz'))
- grad_affine: float32 [9, 65536], P(None, ('gy', 'gz'))
- grad_deform: float32 [9, 65536], P(None, ('gy', 'gz'))
- grad_grip: float32 [2, 2, 3], replicated
The draws below stay inside these ranges and needn't reach their ends.
Inputs may be any that keep to these rules, and one draw needn't show every extreme that they name: cell_index % 128 lies between 1 and 126. `live_count`: a multiple of 128. `deform`: every row's determinant is at least 0.5.
All inputs are finite; a program needn't handle non-finite values.
Results may differ from the reference program's by a relative error of at most 0.0001.
Values sent between devices are 32-bit elements; how exact they have to be, the bound alone decides.
A program may use at most 192 MiB of HBM per device.

```python
import jax
import jax.numpy as jnp
from jax import lax

CX = 128
CY = 16
CZ = 8
PCAP = 2048
SUBSTEPS = 2
GRIPPERS = 2
NY = 64
NZ = 64
PARTS_SIZE = 65536
N_GZ = 8


def draw_deform(key, part):
    spread = jax.random.uniform(key, (9, PARTS_SIZE), jnp.float32, -0.08, 0.08)
    identity = jnp.eye(3, dtype=jnp.float32).reshape(9, 1)
    return identity + spread


def draw_cell_index(key, part):
    key_x, key_y, key_z = jax.random.split(jax.random.fold_in(key, 11), 3)
    cell_x = jax.random.randint(key_x, (PARTS_SIZE,), 1, CX - 1)
    cell_y = jax.random.randint(key_y, (PARTS_SIZE,), 0, CY)
    cell_z = jax.random.randint(key_z, (PARTS_SIZE,), 0, CZ)
    packed = (cell_y * CZ + cell_z) * CX + cell_x
    packed = packed.at[0].set(1).at[PARTS_SIZE - 1].set(CY * CZ * CX - 2)
    return packed.astype(jnp.int32)


def draw_live_count(key, part):
    key_tiles, key_top = jax.random.split(jax.random.fold_in(key, 23))
    device_total = PARTS_SIZE // PCAP
    tiles = jax.random.randint(key_tiles, (device_total,), 1, PCAP // 128 + 1)
    busiest = jax.random.randint(key_top, (), 0, device_total)
    lightest = (busiest + 1) % device_total
    tiles = tiles.at[busiest].set(PCAP // 128).at[lightest].set(1)
    return (tiles * 128).astype(jnp.int32)


def draw_grip_mask(key, part):
    key_hit, key_which = jax.random.split(jax.random.fold_in(key, 37))
    rolled = jax.random.randint(key_hit, (NY, NZ, CX), 0, 60)
    depth = jnp.arange(NZ, dtype=jnp.int32)[None, :, None]
    touched = rolled < 3 + 6 * depth // NZ
    which = jax.random.randint(key_which, (NY, NZ, CX), 1, 3)
    marked = jnp.where(touched, which, 0)
    return marked.at[0, 0, 0].set(2).astype(jnp.int32)


def levels(stream_key, extent, cuts, least, top_value):
    loudness = 1.0
    for axis_at, blocks in cuts:
        steps = jax.random.uniform(jax.random.fold_in(jax.random.fold_in(stream_key, 6), axis_at), (blocks,), jnp.float32, least / len(cuts), top_value / len(cuts))
        loudness = loudness * jnp.repeat(jnp.exp(steps), extent[axis_at] // blocks).reshape((-1,) + (1,) * (len(extent) - 1 - axis_at))
    return loudness


def gaussian(own_key, extent, width, most, shards=(), kind=jnp.bfloat16):
    loudness = levels(own_key, extent, shards, -0.22, 0.18) if shards else 1.0
    values = jax.random.normal(own_key, extent, jnp.float32) * width * loudness
    return jnp.minimum(jnp.maximum(values, -most), most).astype(kind)


def setup_inputs(seed: int = 0) -> dict:
    key_list = jax.random.split(jax.random.key(seed), 13)
    return {
        "offset": jnp.clip(0.6 + 0.79999995 * jax.random.uniform(key_list[0], (3, PARTS_SIZE), jnp.float32) ** levels(key_list[0], (3, PARTS_SIZE), ((1, 32),), -0.2, 0.2), 0.6, 1.4),
        "velocity": gaussian(key_list[1], (3, PARTS_SIZE), 1.0, 4.0, ((1, 32),), jnp.float32),
        "affine": gaussian(key_list[2], (9, PARTS_SIZE), 0.5, 3.0, ((1, 32),), jnp.float32),
        "deform": draw_deform(jax.random.fold_in(key_list[12], 71), 0),
        "cell_index": draw_cell_index(jax.random.fold_in(key_list[12], 71), 0),
        "live_count": draw_live_count(jax.random.fold_in(key_list[12], 71), 0),
        "grip_mask": draw_grip_mask(jax.random.fold_in(key_list[12], 71), 0),
        "grip_velocity": gaussian(key_list[7], (SUBSTEPS, GRIPPERS, 3), 1.0, 4.0, (), jnp.float32),
        "loss_offset": gaussian(key_list[8], (3, PARTS_SIZE), 1.0, 6.0, ((1, 32),), jnp.float32),
        "loss_velocity": gaussian(key_list[9], (3, PARTS_SIZE), 1.0, 6.0, ((1, 32),), jnp.float32),
        "loss_affine": gaussian(key_list[10], (9, PARTS_SIZE), 1.0, 6.0, ((1, 32),), jnp.float32),
        "loss_deform": gaussian(key_list[11], (9, PARTS_SIZE), 1.0, 6.0, ((1, 32),), jnp.float32),
    }


time_step = 0.05
particle_mass = 1.0
shear_modulus = 10.0
bulk_modulus = 10.0
gravity = -2.0
mass_regular = 0.1

def node_offsets(z_extent, x_extent):
    table = []
    for node_y in range(3):
        for node_z in range(3):
            for node_x in range(3):
                table.append((node_y * z_extent + node_z) * x_extent + node_x - 1)
    return jnp.array(table, dtype=jnp.int32)

def spline_nodes(offset):
    spline = (0.5 * (1.5 - offset) ** 2, 0.75 - (offset - 1.0) ** 2, 0.5 * (offset - 0.5) ** 2)
    weights = []
    distance = []
    for node_y in range(3):
        for node_z in range(3):
            for node_x in range(3):
                weights.append(spline[node_x][0] * spline[node_y][1] * spline[node_z][2])
                distance.append(jnp.stack((node_x - offset[0], node_y - offset[1], node_z - offset[2])))
    return (jnp.stack(weights), jnp.stack(distance, axis=1))

def affine_stress(affine, deform):
    deform_mat = deform.reshape(3, 3, -1)
    left_cauchy = 0.0
    for column in range(3):
        left_cauchy = left_cauchy + deform_mat[:, column][:, None, :] * deform_mat[:, column][None, :, :]
    entry = deform_mat
    jacobian = entry[0, 0] * (entry[1, 1] * entry[2, 2] - entry[1, 2] * entry[2, 1]) - entry[0, 1] * (entry[1, 0] * entry[2, 2] - entry[1, 2] * entry[2, 0]) + entry[0, 2] * (entry[1, 0] * entry[2, 1] - entry[1, 1] * entry[2, 0])
    identity = jnp.eye(3, dtype=deform.dtype)[:, :, None]
    kirchhoff = shear_modulus * (left_cauchy - identity) + bulk_modulus * jnp.log(jacobian)[None, None, :] * identity
    return particle_mass * affine.reshape(3, 3, -1) - 4.0 * time_step * kirchhoff

def spread_terms(particle_state, live_rows, node_index, cell_count):
    offset, velocity, affine, deform = particle_state
    weights, distance = spline_nodes(offset)
    affine_mat = affine_stress(affine, deform)
    pushed = particle_mass * velocity[:, None, :]
    for column in range(3):
        pushed = pushed + affine_mat[:, column][:, None, :] * distance[column][None]
    node_momentum = weights[None] * pushed
    node_mass = weights * particle_mass
    terms = jnp.concatenate((node_momentum, node_mass[None]), axis=0) * live_rows
    return jnp.zeros((4, cell_count), terms.dtype).at[:, node_index].add(terms.reshape(4, -1))

def settle_grid(cell_sums, coord_y, coord_z, extent_y, extent_z, grip_mask, grip_now):
    velocity_grid = cell_sums[:3] / (cell_sums[3] + mass_regular)
    lift = jnp.array([0.0, time_step * gravity, 0.0], dtype=cell_sums.dtype)[:, None, None, None]
    velocity_grid = velocity_grid + lift
    sticky = ((coord_y < 3) | (coord_y >= extent_y - 3))[:, None] | ((coord_z < 3) | (coord_z >= extent_z - 3))[None, :]
    velocity_grid = jnp.where(sticky[None, :, :, None], 0.0, velocity_grid)
    for gripper in range(GRIPPERS):
        velocity_grid = jnp.where((grip_mask == gripper + 1)[None], grip_now[gripper][:, None, None, None], velocity_grid)
    return velocity_grid

def gather_state(particle_state, velocity_flat, node_index):
    offset, velocity, affine, deform = particle_state
    weights, distance = spline_nodes(offset)
    row_total = offset.shape[1]
    nearby = velocity_flat[:, node_index].reshape(3, 27, row_total)
    weighted = weights[None] * nearby
    new_velocity = lax.optimization_barrier(jnp.sum(weighted, axis=1))
    new_affine = jnp.stack([4.0 * lax.optimization_barrier(jnp.sum(weighted * distance[column][None], axis=1)) for column in range(3)], axis=1)
    new_offset = offset + time_step * new_velocity
    deform_mat = deform.reshape(3, 3, row_total)
    new_deform = deform_mat
    for column in range(3):
        new_deform = new_deform + time_step * new_affine[:, column][:, None, :] * deform_mat[column][None]
    return (new_offset, new_velocity, new_affine.reshape(9, row_total), new_deform.reshape(9, row_total))

def reference(offset, velocity, affine, deform, cell_index, live_count, grip_mask, grip_velocity, loss_offset, loss_velocity, loss_affine, loss_deform):
    row_ids = jnp.arange(offset.shape[1], dtype=jnp.int32)
    device = row_ids // PCAP
    live_rows = (row_ids % PCAP < live_count[device]).astype(offset.dtype)
    cell_x = cell_index % CX
    remainder = cell_index // CX
    global_y = device // N_GZ * CY + remainder // CZ
    global_z = device % N_GZ * CZ + remainder % CZ
    first_index = (global_y * (NZ + 2) + global_z) * CX + cell_x
    node_index = (node_offsets(NZ + 2, CX)[:, None] + first_index[None, :]).reshape(-1).astype(jnp.int32)
    coord_y = jnp.arange(NY, dtype=jnp.int32)
    coord_z = jnp.arange(NZ, dtype=jnp.int32)
    cell_count = (NY + 2) * (NZ + 2) * CX

    def advance(particle_state, grip_now):
        grid_sum = spread_terms(particle_state, live_rows, node_index, cell_count).reshape(4, NY + 2, NZ + 2, CX)
        cell_sums = grid_sum[:, 1:NY + 1, 1:NZ + 1]
        velocity_grid = settle_grid(cell_sums, coord_y, coord_z, NY, NZ, grip_mask, grip_now)
        padded = jnp.pad(velocity_grid, ((0, 0), (1, 1), (1, 1), (0, 0)))
        return gather_state(particle_state, padded.reshape(3, -1), node_index)

    def forward(particle_state, grips):
        for substep in range(SUBSTEPS):
            particle_state = advance(particle_state, grips[substep])
        return particle_state
    initial = (offset, velocity, affine, deform)
    final_state, pullback = jax.vjp(forward, initial, grip_velocity)
    seeds = tuple((member * live_rows for member in (loss_offset, loss_velocity, loss_affine, loss_deform)))
    grads, grad_grip = pullback(seeds)
    return (grads[0], grads[1], grads[2], grads[3], grad_grip)
```

```python
import functools

import jax
import jax.numpy as jnp
from jax import lax
from jax.experimental import pallas as pl
from jax.experimental.pallas import tpu as pltpu
from jax.sharding import PartitionSpec as P

DT = 0.05
SHEAR = 10.0
BULK = 10.0
GRAVITY = -2.0
MASS_REG = 0.1
F32 = jnp.float32
BF16 = jnp.bfloat16
MESH = pl.DeviceIdType.MESH
DIRS = [(-1, -1), (-1, 0), (-1, 1), (0, -1), (0, 1), (1, -1), (1, 0), (1, 1)]
YB = 4
COMPS = (5, 4, 3, 3)


def splines(f):
    return (0.5 * (1.5 - f) ** 2, 0.75 - (f - 1.0) ** 2, 0.5 * (f - 0.5) ** 2)


def dsplines(f):
    return (f - 1.5, -2.0 * (f - 1.0), f - 0.5)


def pick3(b, vals):
    return jnp.where(b == 0, vals[0], jnp.where(b == 1, vals[1], jnp.where(b == 2, vals[2], 0.0)))


def sub_sum(x):
    return jnp.sum(x, axis=0, keepdims=True)


def split(x):
    hi = x.astype(BF16)
    lo = (x - hi.astype(F32)).astype(BF16)
    return hi, lo


def stress(c_rows, f_rows):
    f = f_rows
    cof = [
        f[4] * f[8] - f[5] * f[7],
        f[5] * f[6] - f[3] * f[8],
        f[3] * f[7] - f[4] * f[6],
        f[2] * f[7] - f[1] * f[8],
        f[0] * f[8] - f[2] * f[6],
        f[1] * f[6] - f[0] * f[7],
        f[1] * f[5] - f[2] * f[4],
        f[2] * f[3] - f[0] * f[5],
        f[0] * f[4] - f[1] * f[3],
    ]
    det = f[0] * cof[0] + f[1] * cof[1] + f[2] * cof[2]
    log_det = jnp.log(det)
    a_rows = []
    for i in range(3):
        for j in range(3):
            left = f[3 * i] * f[3 * j] + f[3 * i + 1] * f[3 * j + 1] + f[3 * i + 2] * f[3 * j + 2]
            tau = SHEAR * (left - 1.0) + BULK * log_det if i == j else SHEAR * left
            a_rows.append(c_rows[3 * i + j] - 4.0 * DT * tau)
    return a_rows, det, cof


def kernel(
    ny, nz, span_y, span_z, span_x, rows, chunk,
    off_ref, vel_ref, aff_ref, def_ref, idx_ref, live_ref, mask_ref, grip_ref,
    lo_ref, lv_ref, la_ref, ld_ref,
    go_ref, gv_ref, ga_ref, gd_ref, gg_ref,
    oh, oht, acc, grid, ybuf, sums, maskx, u_hi, u_lo, node, node_b,
    off1, vel1, aff1, def1, aff2, vel2, up_o, up_v, up_a, up_d,
    rz, ry, rc, gsend, gbuf1, gsend2, gbuf2,
    send_sem, recv_sem, gs1, gr1, gs2, gr2,
):
    me_y = lax.axis_index("gy")
    me_z = lax.axis_index("gz")
    zr = span_z + 2
    bands = span_y // YB
    yp = grid.shape[2]
    zbits = span_z.bit_length() - 1
    xbits = span_x.bit_length() - 1
    steps = rows // chunk

    barrier = pltpu.get_barrier_semaphore()

    @pl.loop(1, nz)
    def _(d):
        pl.semaphore_signal(barrier, inc=1, device_id=(me_y, lax.rem(me_z + d, nz)), device_id_type=MESH)

    @pl.loop(1, ny)
    def _(d):
        pl.semaphore_signal(barrier, inc=1, device_id=(lax.rem(me_y + d, ny), me_z), device_id_type=MESH)

    def exists(d):
        dy, dz = DIRS[d]
        ok = None
        if dy:
            ok = me_y > 0 if dy < 0 else me_y < ny - 1
        if dz:
            okz = me_z > 0 if dz < 0 else me_z < nz - 1
            ok = okz if ok is None else jnp.logical_and(ok, okz)
        return ok

    for d in (0, 2, 5, 7):
        @pl.when(exists(d))
        def _():
            pl.semaphore_signal(
                barrier, inc=1, device_id=(me_y + DIRS[d][0], me_z + DIRS[d][1]), device_id_type=MESH
            )

    def barrier_wait():
        sides_y = (me_y > 0).astype(jnp.int32) + (me_y < ny - 1).astype(jnp.int32)
        sides_z = (me_z > 0).astype(jnp.int32) + (me_z < nz - 1).astype(jnp.int32)
        pl.semaphore_wait(barrier, ny + nz - 2 + sides_y * sides_z)

    def column(sl):
        idx = idx_ref[:, sl]
        rem = idx >> xbits
        return ((rem >> (zbits + 2)) << xbits) + (idx & (span_x - 1))

    @pl.loop(0, steps)
    def _(s):
        sl = pl.ds(pl.multiple_of(s * chunk, chunk), chunk)
        col = column(sl)
        wide = bands * span_x
        rows_iota = lax.broadcasted_iota(jnp.int32, (wide, chunk), 0)
        oh[:, sl] = jnp.where(rows_iota == col, 1.0, 0.0).astype(BF16)
        col_t = jnp.transpose(jnp.broadcast_to(col.astype(F32), (128, chunk)))
        lane = lax.broadcasted_iota(jnp.int32, (chunk, 128), 1)
        for part in range(wide // 128):
            oht[sl, part * 128:(part + 1) * 128] = jnp.where(
                col_t == (lane + part * 128).astype(F32), 1.0, 0.0
            ).astype(BF16)

    def geometry(sl):
        rem = idx_ref[:, sl] >> xbits
        pz = rem & (span_z - 1)
        yl = (rem >> zbits) & (YB - 1)
        b = lax.broadcasted_iota(jnp.int32, (8, chunk), 0) - yl
        return pz, b

    def live_of(s):
        lane = lax.broadcasted_iota(jnp.int32, (1, chunk), 1) + s * chunk
        return jnp.where(lane < live_ref[0], 1.0, 0.0)

    def row_list(ref, sl):
        return [ref[i:i + 1, sl] for i in range(ref.shape[0])]

    def scatter_chunk(s, sl, f, v, a_mat, scale, mass):
        pz, b = geometry(sl)
        wx = splines(f[0])
        ex = [k - f[0] for k in range(3)]
        wy = pick3(b, splines(f[1]))
        if scale is not None:
            wy = wy * scale
        ey = b.astype(F32) - f[1]
        sz = splines(f[2])
        c = [z - pz for z in range(zr)]
        wyz = [wy * pick3(c[z], sz) for z in range(zr)]
        ez = [c[z].astype(F32) - f[2] for z in range(zr)]
        his, los = [], []
        for i in range(3):
            vy = v[i] + a_mat[3 * i + 1] * ey
            t = [wyz[z] * (vy + a_mat[3 * i + 2] * ez[z]) for z in range(zr)]
            for a in range(3):
                coef = wx[a] * (a_mat[3 * i] * ex[a])
                block = jnp.concatenate([t[z] * wx[a] + wyz[z] * coef for z in range(zr)], axis=0)
                hi, lo = split(block)
                his.append(hi)
                los.append(lo)
        if mass:
            for a in range(3):
                block = jnp.concatenate([wyz[z] * wx[a] for z in range(zr)], axis=0)
                hi, lo = split(block)
                his.append(hi)
                los.append(lo)
        hot = oht[sl, :]
        for i in range(4 if mass else 3):
            hi = jnp.concatenate(his[3 * i:3 * i + 3], axis=0)
            lo = jnp.concatenate(los[3 * i:3 * i + 3], axis=0)
            part = jnp.dot(hi, hot, preferred_element_type=F32)
            part = part + jnp.dot(lo, hot, preferred_element_type=F32)
            height = 3 * zr * 8
            acc[i * height:(i + 1) * height, :] += part

    def fold(comps):
        for i in range(comps):
            bands_out = []
            for h in range(bands):
                total = None
                for a in range(3):
                    at = (3 * i + a) * zr * 8
                    piece = acc[at:at + zr * 8, h * span_x:(h + 1) * span_x]
                    if a != 1:
                        piece = pltpu.roll(piece, (a - 1) % span_x, 1)
                    total = piece if total is None else total + piece
                bands_out.append(total.reshape(zr, 8, span_x))
            for h in range(0, bands, 2):
                grid[i, :, h * YB:h * YB + 8, :] = bands_out[h]
            grid[i, :, bands * YB:, :] = jnp.zeros((zr, yp - bands * YB, span_x), F32)
            for h in range(1, bands, 2):
                grid[i, :, h * YB:h * YB + 8, :] += bands_out[h]

    def slab(d, n):
        dy, dz = DIRS[d]
        zs = pl.ds(0, 2) if dz < 0 else pl.ds(zr - 2, 2)
        side = 0 if dy < 0 else 1
        if dy == 0:
            return grid.at[pl.ds(0, n), zs]
        if dz == 0:
            return ybuf.at[side, pl.ds(0, n)]
        return ybuf.at[side, pl.ds(0, n), zs]

    def landing(e, d, n):
        dy, dz = DIRS[d]
        if dy == 0:
            return rz.at[e, 0 if dz < 0 else 1, pl.ds(0, n)]
        if dz == 0:
            return ry.at[e, 0 if dy < 0 else 1, pl.ds(0, n)]
        return rc.at[e, (0 if dy < 0 else 2) + (0 if dz < 0 else 1), pl.ds(0, n)]

    def exchange(e, out):
        n = COMPS[e]
        ybuf[0, 0:n] = grid[0:n, :, 0:2, :]
        ybuf[1, 0:n] = grid[0:n, :, span_y:span_y + 2, :]
        order = (3, 4, 1, 6, 0, 2, 5, 7)
        for d in order:
            @pl.when(exists(d))
            def _():
                pltpu.make_async_remote_copy(
                    src_ref=slab(d, n), dst_ref=landing(e, 7 - d, n),
                    send_sem=send_sem.at[e, d], recv_sem=recv_sem.at[e, 7 - d],
                    device_id=(me_y + DIRS[d][0], me_z + DIRS[d][1]), device_id_type=MESH,
                ).start()
        for i in range(n):
            out(i)[...] = grid[i]
        for d in order:
            dy, dz = DIRS[d]

            @pl.when(exists(d))
            def _():
                copy = pltpu.make_async_remote_copy(
                    src_ref=slab(d, n), dst_ref=landing(e, d, n),
                    send_sem=send_sem.at[e, d], recv_sem=recv_sem.at[e, d],
                    device_id=(me_y + dy, me_z + dz), device_id_type=MESH,
                )
                copy.wait_recv()
                zs = slice(0, zr) if dz == 0 else (slice(0, 2) if dz < 0 else slice(zr - 2, zr))
                ys = slice(0, yp) if dy == 0 else (slice(0, 2) if dy < 0 else slice(span_y, span_y + 2))
                landed = landing(e, d, n)
                for i in range(n):
                    out(i)[zs, ys, :] += landed[i]
                copy.wait_send()

    def cell_kinds():
        shape = (zr, yp, span_x)
        gy = lax.broadcasted_iota(jnp.int32, shape, 1) - 1 + me_y * span_y
        gz = lax.broadcasted_iota(jnp.int32, shape, 0) - 1 + me_z * span_z
        sticky = (gy < 3) | (gy >= ny * span_y - 3) | (gz < 3) | (gz >= nz * span_z - 3)
        return sticky, maskx[...]

    def put_u(i, value):
        for a in range(3):
            turned = value.reshape(zr * yp, span_x)
            if a != 1:
                turned = pltpu.roll(turned, (1 - a) % span_x, 1)
            turned = turned.reshape(zr, yp, span_x)
            at = (3 * i + a) * zr * 8
            for h in range(bands):
                hi, lo = split(turned[:, h * YB:h * YB + 8, :].reshape(zr * 8, span_x))
                u_hi[at:at + zr * 8, h * span_x:(h + 1) * span_x] = hi
                u_lo[at:at + zr * 8, h * span_x:(h + 1) * span_x] = lo

    def settle(e):
        sticky, kind = cell_kinds()
        inv = 1.0 / (sums[e, 3] + MASS_REG)
        for i in range(3):
            u = sums[e, i] * inv
            if i == 1:
                u = u + DT * GRAVITY
            u = jnp.where(sticky, 0.0, u)
            for k in range(2):
                u = jnp.where(kind == float(k + 1), grip_ref[(e * 2 + k) * 3 + i], u)
            put_u(i, u)

    def settle_back(e):
        sticky, kind = cell_kinds()
        free = jnp.logical_and(jnp.logical_not(sticky), kind == 0.0)
        inv = 1.0 / (sums[e, 3] + MASS_REG)
        mass = None
        for i in range(3):
            gu = sums[2, i]
            for k in range(2):
                hit = jnp.where(kind == float(k + 1), gu, 0.0)
                part = jnp.sum(hit[1:span_z + 1], axis=0)
                part = sub_sum(part[1:span_y + 1])
                gsend[e, 3 * k + i:3 * k + i + 1, :] = part
            gs = jnp.where(free, gu * inv, 0.0)
            term = gs * sums[e, i]
            mass = term if mass is None else mass + term
            put_u(i, gs)
        put_u(3, -mass * inv)

    def gather_chunk(sl, comps):
        pz, b = geometry(sl)
        hot = oh[:, sl]
        bits = [(pz & (1 << k)) != 0 for k in range(zbits)]
        out = []
        for i in range(comps):
            for a in range(3):
                at = (3 * i + a) * zr * 8
                h = jnp.dot(u_hi[at:at + zr * 8, :], hot, preferred_element_type=F32)
                h = h + jnp.dot(u_lo[at:at + zr * 8, :], hot, preferred_element_type=F32)
                vals = [h[z * 8:(z + 1) * 8] for z in range(zr)]
                for k in reversed(range(zbits)):
                    shift = 1 << k
                    vals = [
                        jnp.where(bits[k], vals[z + shift], vals[z]) for z in range(len(vals) - shift)
                    ]
                out.append(vals)
        return out

    def moments(vals, f, b):
        wx = splines(f[0])
        wz = splines(f[2])
        wex = [wx[a] * (a - f[0]) for a in range(3)]
        wez = [wz[c] * (c - f[2]) for c in range(3)]
        wy = pick3(b, splines(f[1]))
        wey = wy * (b.astype(F32) - f[1])
        plain, first = [], []
        for i in range(3):
            x0 = [sum(wx[a] * vals[3 * i + a][c] for a in range(3)) for c in range(3)]
            x1 = [sum(wex[a] * vals[3 * i + a][c] for a in range(3)) for c in range(3)]
            z00 = sum(wz[c] * x0[c] for c in range(3))
            z10 = sum(wz[c] * x1[c] for c in range(3))
            z01 = sum(wez[c] * x0[c] for c in range(3))
            plain.append(sub_sum(wy * z00))
            first += [sub_sum(wy * z10), sub_sum(wey * z00), sub_sum(wy * z01)]
        return plain, first

    def weight_pull(vals, f, b, g, d_mat, extra):
        wx, dx = splines(f[0]), dsplines(f[0])
        wz, dz = splines(f[2]), dsplines(f[2])
        wy = pick3(b, splines(f[1]))
        dy = pick3(b, dsplines(f[1]))
        ey = b.astype(F32) - f[1]
        k_rows = [g[i] + d_mat[3 * i + 1] * ey for i in range(3)]
        by_x = [[d_mat[3 * i] * (a - f[0]) for a in range(3)] for i in range(3)]
        by_z = [[d_mat[3 * i + 2] * (c - f[2]) for c in range(3)] for i in range(3)]
        s_x = s_y = s_z = 0.0
        for c in range(3):
            q_w = q_d = 0.0
            for a in range(3):
                q = sum(vals[3 * i + a][c] * (k_rows[i] + (by_x[i][a] + by_z[i][c])) for i in range(3))
                if extra:
                    q = q + vals[9 + a][c]
                q_w = q_w + wx[a] * q
                q_d = q_d + dx[a] * q
            s_x = s_x + wz[c] * q_d
            s_y = s_y + wz[c] * q_w
            s_z = s_z + dz[c] * q_w
        return [sub_sum(wy * s_x), sub_sum(dy * s_y), sub_sum(wy * s_z)]

    states = ((off_ref, vel_ref, aff_ref, def_ref), (off1, vel1, aff1, def1))
    afters = ((off1, vel1, aff1, def1), (None, vel2, aff2, None))

    def forward(e):
        o_r, v_r, a_r, d_r = states[e]
        acc[...] = jnp.zeros_like(acc)

        @pl.loop(0, steps)
        def _(s):
            sl = pl.ds(pl.multiple_of(s * chunk, chunk), chunk)
            a_mat, _, _ = stress(row_list(a_r, sl), row_list(d_r, sl))
            scatter_chunk(s, sl, row_list(o_r, sl), row_list(v_r, sl), a_mat, live_of(s), True)

        fold(4)
        if e == 0:
            grid[4] = jnp.zeros((zr, yp, span_x), F32)
            for z in range(span_z):
                grid[4, z + 1, 1:span_y + 1, :] = mask_ref[:, z, :].astype(F32)
            barrier_wait()
        exchange(e, lambda i: sums.at[e, i] if i < 4 else maskx)
        settle(e)
        n_o, n_v, n_a, n_d = afters[e]

        @pl.loop(0, steps)
        def _(s):
            sl = pl.ds(pl.multiple_of(s * chunk, chunk), chunk)
            _, b = geometry(sl)
            f = row_list(o_r, sl)
            vals = gather_chunk(sl, 3)
            for r in range(9):
                for c in range(3):
                    node[e, 3 * r + c, :, sl] = vals[r][c]
            plain, first = moments(vals, f, b)
            new_a = [4.0 * m for m in first]
            for i in range(3):
                n_v[i:i + 1, sl] = plain[i]
            for i in range(9):
                n_a[i:i + 1, sl] = new_a[i]
            if n_o is not None:
                dm = row_list(d_r, sl)
                for i in range(3):
                    n_o[i:i + 1, sl] = f[i] + DT * plain[i]
                for i in range(3):
                    for k in range(3):
                        n_d[3 * i + k:3 * i + k + 1, sl] = dm[3 * i + k] + DT * sum(
                            new_a[3 * i + j] * dm[3 * j + k] for j in range(3)
                        )

    def gather_seeds(e, s, sl, dm):
        if e == 1:
            live = live_of(s)
            up = [[live * r for r in row_list(ref, sl)] for ref in (lo_ref, lv_ref, la_ref, ld_ref)]
        else:
            up = [row_list(ref, sl) for ref in (up_o, up_v, up_a, up_d)]
        g_o, g_v, g_a, g_d = up
        g = [g_v[i] + DT * g_o[i] for i in range(3)]
        d_mat = [
            4.0 * (g_a[3 * i + j] + DT * sum(g_d[3 * i + k] * dm[3 * j + k] for k in range(3)))
            for i in range(3)
            for j in range(3)
        ]
        return g_o, g_d, g, d_mat

    def backward(e, before, between):
        o_r, v_r, a_r, d_r = states[e]
        n_v, n_a = afters[e][1], afters[e][2]
        acc[...] = jnp.zeros_like(acc)

        @pl.loop(0, steps)
        def _(s):
            sl = pl.ds(pl.multiple_of(s * chunk, chunk), chunk)
            _, _, g, d_mat = gather_seeds(e, s, sl, row_list(d_r, sl))
            scatter_chunk(s, sl, row_list(o_r, sl), g, d_mat, None, False)

        fold(3)
        exchange(3 - e, lambda i: sums.at[2, i])
        settle_back(e)
        before()
        outs = (up_o, up_v, up_a, up_d) if e == 1 else (go_ref, gv_ref, ga_ref, gd_ref)

        def body(s):
            sl = pl.ds(pl.multiple_of(s * chunk, chunk), chunk)
            _, b = geometry(sl)
            live = live_of(s)
            f = row_list(o_r, sl)
            dm = row_list(d_r, sl)
            g_o, g_d, g, d_mat = gather_seeds(e, s, sl, dm)
            held = [[node[e, 3 * r + c, :, sl] for c in range(3)] for r in range(9)]
            pull = weight_pull(held, f, b, g, d_mat, False)
            vn = row_list(n_v, sl)
            cn = row_list(n_a, sl)
            grad_o = [
                g_o[k] + pull[k] - sum(d_mat[3 * i + k] * vn[i] for i in range(3)) for k in range(3)
            ]
            grad_d = [
                g_d[3 * j + k] + DT * sum(cn[3 * i + j] * g_d[3 * i + k] for i in range(3))
                for j in range(3)
                for k in range(3)
            ]
            vals = gather_chunk(sl, 4)
            plain, first = moments(vals, f, b)
            grad_v = [live * m for m in plain]
            grad_a = [live * m for m in first]
            a_mat, det, cof = stress(row_list(a_r, sl), dm)
            pull = weight_pull(vals, f, b, row_list(v_r, sl), a_mat, True)
            for k in range(3):
                outs[0][k:k + 1, sl] = grad_o[k] + live * pull[k] - sum(
                    a_mat[3 * i + k] * grad_v[i] for i in range(3)
                )
                outs[1][k:k + 1, sl] = grad_v[k]
            scale = (-4.0 * DT * BULK) * (grad_a[0] + grad_a[4] + grad_a[8]) / det
            for i in range(3):
                for k in range(3):
                    sym = sum((grad_a[3 * i + j] + grad_a[3 * j + i]) * dm[3 * j + k] for j in range(3))
                    at = 3 * i + k
                    outs[2][at:at + 1, sl] = grad_a[at]
                    outs[3][at:at + 1, sl] = grad_d[at] + (-4.0 * DT * SHEAR) * sym + scale * cof[at]

        pl.loop(0, steps // 2)(body)
        between()
        pl.loop(steps // 2, steps)(body)

    def grip_copy(axis, n, me, peer, slot, src, buf, ssem, rsem):
        device = (me_y, peer) if axis == "gz" else (peer, me_z)
        return pltpu.make_async_remote_copy(
            src_ref=src, dst_ref=buf.at[slot], send_sem=ssem.at[peer], recv_sem=rsem.at[slot],
            device_id=device, device_id_type=MESH,
        )

    def grip_start(axis, n, me, src, buf, ssem, rsem):
        buf[pl.ds(me, 1)] = src[...][None]

        @pl.loop(1, n)
        def _(d):
            grip_copy(axis, n, me, lax.rem(me + d, n), me, src, buf, ssem, rsem).start()

    def grip_finish(axis, n, me, src, buf, ssem, rsem):
        @pl.loop(1, n)
        def _(d):
            peer = lax.rem(me + d, n)
            copy = grip_copy(axis, n, me, peer, peer, src, buf, ssem, rsem)
            copy.wait_recv()
            copy.wait_send()

        total = buf[0]
        for at in range(1, n):
            total = total + buf[at]
        return total

    stage1 = ("gz", nz, me_z, gsend, gbuf1, gs1, gr1)
    stage2 = ("gy", ny, me_y, gsend2, gbuf2, gs2, gr2)

    def between_last():
        gsend2[...] = grip_finish(*stage1)
        grip_start(*stage2)

    def nothing():
        return None

    gsend[...] = jnp.zeros_like(gsend)
    forward(0)
    forward(1)
    backward(1, nothing, nothing)
    backward(0, lambda: grip_start(*stage1), between_last)
    total = grip_finish(*stage2)
    gg_ref[...] = jnp.broadcast_to(jnp.sum(total, axis=2, keepdims=True), total.shape)


def shards(ny, nz, offset, velocity, affine, deform, cell_index, live_count, grip_mask, grip_velocity,
           loss_offset, loss_velocity, loss_affine, loss_deform):
    span_y, span_z, span_x = grip_mask.shape
    rows = offset.shape[1]
    chunk = 256
    zr = span_z + 2
    bands = span_y // YB
    yp = (span_y + 2 + 7) // 8 * 8
    wide = bands * span_x
    vmem = pl.BlockSpec(memory_space=pltpu.VMEM)
    smem = pl.BlockSpec(memory_space=pltpu.SMEM)
    shape = jax.ShapeDtypeStruct
    scratch = [
        pltpu.VMEM((wide, rows), BF16),
        pltpu.VMEM((rows, wide), BF16),
        pltpu.VMEM((12 * zr * 8, wide), F32),
        pltpu.VMEM((5, zr, yp, span_x), F32),
        pltpu.VMEM((2, 5, zr, 2, span_x), F32),
        pltpu.VMEM((3, 4, zr, yp, span_x), F32),
        pltpu.VMEM((zr, yp, span_x), F32),
        pltpu.VMEM((12 * zr * 8, wide), BF16),
        pltpu.VMEM((12 * zr * 8, wide), BF16),
        pltpu.VMEM((2, 27, 8, rows), F32),
        pltpu.VMEM((8, 128), F32),
        pltpu.VMEM((3, rows), F32),
        pltpu.VMEM((3, rows), F32),
        pltpu.VMEM((9, rows), F32),
        pltpu.VMEM((9, rows), F32),
        pltpu.VMEM((9, rows), F32),
        pltpu.VMEM((3, rows), F32),
        pltpu.VMEM((3, rows), F32),
        pltpu.VMEM((3, rows), F32),
        pltpu.VMEM((9, rows), F32),
        pltpu.VMEM((9, rows), F32),
        pltpu.VMEM((4, 2, 5, 2, yp, span_x), F32),
        pltpu.VMEM((4, 2, 5, zr, 2, span_x), F32),
        pltpu.VMEM((4, 4, 5, 2, 2, span_x), F32),
        pltpu.VMEM((2, 8, span_x), F32),
        pltpu.VMEM((nz, 2, 8, span_x), F32),
        pltpu.VMEM((2, 8, span_x), F32),
        pltpu.VMEM((ny, 2, 8, span_x), F32),
        pltpu.SemaphoreType.DMA((4, 8)),
        pltpu.SemaphoreType.DMA((4, 8)),
        pltpu.SemaphoreType.DMA((nz,)),
        pltpu.SemaphoreType.DMA((nz,)),
        pltpu.SemaphoreType.DMA((ny,)),
        pltpu.SemaphoreType.DMA((ny,)),
    ]
    outs = pl.pallas_call(
        functools.partial(kernel, ny, nz, span_y, span_z, span_x, rows, chunk),
        out_shape=(
            shape((3, rows), F32), shape((3, rows), F32), shape((9, rows), F32), shape((9, rows), F32),
            shape((2, 8, span_x), F32),
        ),
        in_specs=[vmem, vmem, vmem, vmem, vmem, smem, vmem, smem, vmem, vmem, vmem, vmem],
        out_specs=(vmem,) * 5,
        scratch_shapes=scratch,
        compiler_params=pltpu.CompilerParams(
            collective_id=0, has_side_effects=True, vmem_limit_bytes=56 * 1024 * 1024
        ),
    )(offset, velocity, affine, deform, cell_index.reshape(1, rows), live_count, grip_mask,
      grip_velocity.reshape(-1), loss_offset, loss_velocity, loss_affine, loss_deform)
    grad_grip = outs[4][:, :6, 0].reshape(2, 2, 3)
    return (outs[0], outs[1], outs[2], outs[3], grad_grip)


def solution(mesh):
    rows = P(None, ("gy", "gz"))
    ny, nz = mesh.shape["gy"], mesh.shape["gz"]
    return jax.shard_map(
        functools.partial(shards, ny, nz),
        mesh=mesh,
        in_specs=(
            rows, rows, rows, rows, P(("gy", "gz")), P(("gy", "gz")), P("gy", "gz", None), P(),
            rows, rows, rows, rows,
        ),
        out_specs=(rows, rows, rows, rows, P()),
        check_vma=False,
    )
```

```python
import functools

import jax
import jax.numpy as jnp
from jax import lax
from jax.experimental import pallas as pl
from jax.experimental.pallas import tpu as pltpu
from jax.sharding import PartitionSpec as P

DT = 0.05
SHEAR = 10.0
BULK = 10.0
GRAVITY = -2.0
MASS_REG = 0.1
F32 = jnp.float32
BF16 = jnp.bfloat16
MESH = pl.DeviceIdType.MESH
DIRS = [(-1, -1), (-1, 0), (-1, 1), (0, -1), (0, 1), (1, -1), (1, 0), (1, 1)]
YB = 4
COMPS = (5, 4, 3, 3)


def splines(f):
    return (0.5 * (1.5 - f) ** 2, 0.75 - (f - 1.0) ** 2, 0.5 * (f - 0.5) ** 2)


def dsplines(f):
    return (f - 1.5, -2.0 * (f - 1.0), f - 0.5)


def pick3(b, vals):
    return jnp.where(b == 0, vals[0], jnp.where(b == 1, vals[1], jnp.where(b == 2, vals[2], 0.0)))


def sub_sum(x):
    return jnp.sum(x, axis=0, keepdims=True)


def split(x):
    hi = x.astype(BF16)
    lo = (x - hi.astype(F32)).astype(BF16)
    return hi, lo


def stress(c_rows, f_rows):
    f = f_rows
    cof = [
        f[4] * f[8] - f[5] * f[7],
        f[5] * f[6] - f[3] * f[8],
        f[3] * f[7] - f[4] * f[6],
        f[2] * f[7] - f[1] * f[8],
        f[0] * f[8] - f[2] * f[6],
        f[1] * f[6] - f[0] * f[7],
        f[1] * f[5] - f[2] * f[4],
        f[2] * f[3] - f[0] * f[5],
        f[0] * f[4] - f[1] * f[3],
    ]
    det = f[0] * cof[0] + f[1] * cof[1] + f[2] * cof[2]
    log_det = jnp.log(det)
    a_rows = []
    for i in range(3):
        for j in range(3):
            left = f[3 * i] * f[3 * j] + f[3 * i + 1] * f[3 * j + 1] + f[3 * i + 2] * f[3 * j + 2]
            tau = SHEAR * (left - 1.0) + BULK * log_det if i == j else SHEAR * left
            a_rows.append(c_rows[3 * i + j] - 4.0 * DT * tau)
    return a_rows, det, cof


def kernel(
    ny, nz, span_y, span_z, span_x, rows, chunk,
    off_ref, vel_ref, aff_ref, def_ref, idx_ref, live_ref, mask_ref, grip_ref,
    lo_ref, lv_ref, la_ref, ld_ref,
    go_ref, gv_ref, ga_ref, gd_ref, gg_ref,
    oh, oht, acc, grid, ybuf, sums, maskx, u_hi, u_lo, node, node_b,
    off1, vel1, aff1, def1, aff2, vel2, up_o, up_v, up_a, up_d,
    rz, ry, rc, gsend, gbuf1, gsend2, gbuf2,
    send_sem, recv_sem, gs1, gr1, gs2, gr2,
):
    me_y = lax.axis_index("gy")
    me_z = lax.axis_index("gz")
    zr = span_z + 2
    bands = span_y // YB
    yp = grid.shape[2]
    zbits = span_z.bit_length() - 1
    xbits = span_x.bit_length() - 1
    steps = rows // chunk

    barrier = pltpu.get_barrier_semaphore()

    @pl.loop(1, nz)
    def _(d):
        pl.semaphore_signal(barrier, inc=1, device_id=(me_y, lax.rem(me_z + d, nz)), device_id_type=MESH)

    @pl.loop(1, ny)
    def _(d):
        pl.semaphore_signal(barrier, inc=1, device_id=(lax.rem(me_y + d, ny), me_z), device_id_type=MESH)

    def exists(d):
        dy, dz = DIRS[d]
        ok = None
        if dy:
            ok = me_y > 0 if dy < 0 else me_y < ny - 1
        if dz:
            okz = me_z > 0 if dz < 0 else me_z < nz - 1
            ok = okz if ok is None else jnp.logical_and(ok, okz)
        return ok

    for d in (0, 2, 5, 7):
        @pl.when(exists(d))
        def _():
            pl.semaphore_signal(
                barrier, inc=1, device_id=(me_y + DIRS[d][0], me_z + DIRS[d][1]), device_id_type=MESH
            )

    def barrier_wait():
        sides_y = (me_y > 0).astype(jnp.int32) + (me_y < ny - 1).astype(jnp.int32)
        sides_z = (me_z > 0).astype(jnp.int32) + (me_z < nz - 1).astype(jnp.int32)
        pl.semaphore_wait(barrier, ny + nz - 2 + sides_y * sides_z)

    def column(sl):
        idx = idx_ref[:, sl]
        rem = idx >> xbits
        return ((rem >> (zbits + 2)) << xbits) + (idx & (span_x - 1))

    @pl.loop(0, steps)
    def _(s):
        sl = pl.ds(pl.multiple_of(s * chunk, chunk), chunk)
        col = column(sl)
        wide = bands * span_x
        rows_iota = lax.broadcasted_iota(jnp.int32, (wide, chunk), 0)
        oh[:, sl] = jnp.where(rows_iota == col, 1.0, 0.0).astype(BF16)
        col_t = jnp.transpose(jnp.broadcast_to(col.astype(F32), (128, chunk)))
        lane = lax.broadcasted_iota(jnp.int32, (chunk, 128), 1)
        for part in range(wide // 128):
            oht[sl, part * 128:(part + 1) * 128] = jnp.where(
                col_t == (lane + part * 128).astype(F32), 1.0, 0.0
            ).astype(BF16)

    def geometry(sl):
        rem = idx_ref[:, sl] >> xbits
        pz = rem & (span_z - 1)
        yl = (rem >> zbits) & (YB - 1)
        b = lax.broadcasted_iota(jnp.int32, (8, chunk), 0) - yl
        return pz, b

    def live_of(s):
        lane = lax.broadcasted_iota(jnp.int32, (1, chunk), 1) + s * chunk
        return jnp.where(lane < live_ref[0], 1.0, 0.0)

    def row_list(ref, sl):
        return [ref[i:i + 1, sl] for i in range(ref.shape[0])]

    def scatter_chunk(s, sl, f, v, a_mat, scale, mass):
        pz, b = geometry(sl)
        wx = splines(f[0])
        ex = [k - f[0] for k in range(3)]
        wy = pick3(b, splines(f[1]))
        if scale is not None:
            wy = wy * scale
        ey = b.astype(F32) - f[1]
        sz = splines(f[2])
        c = [z - pz for z in range(zr)]
        wyz = [wy * pick3(c[z], sz) for z in range(zr)]
        ez = [c[z].astype(F32) - f[2] for z in range(zr)]
        his, los = [], []
        for i in range(3):
            vy = v[i] + a_mat[3 * i + 1] * ey
            t = [wyz[z] * (vy + a_mat[3 * i + 2] * ez[z]) for z in range(zr)]
            for a in range(3):
                coef = wx[a] * (a_mat[3 * i] * ex[a])
                block = jnp.concatenate([t[z] * wx[a] + wyz[z] * coef for z in range(zr)], axis=0)
                hi, lo = split(block)
                his.append(hi)
                los.append(lo)
        if mass:
            for a in range(3):
                block = jnp.concatenate([wyz[z] * wx[a] for z in range(zr)], axis=0)
                hi, lo = split(block)
                his.append(hi)
                los.append(lo)
        hot = oht[sl, :]
        total = (12 if mass else 9) * zr * 8
        part = jnp.dot(jnp.concatenate(his, axis=0), hot, preferred_element_type=F32)
        part = part + jnp.dot(jnp.concatenate(los, axis=0), hot, preferred_element_type=F32)
        acc[0:total, :] += part

    def fold(comps):
        for i in range(comps):
            bands_out = []
            for h in range(bands):
                total = None
                for a in range(3):
                    at = (3 * i + a) * zr * 8
                    piece = acc[at:at + zr * 8, h * span_x:(h + 1) * span_x]
                    if a != 1:
                        piece = pltpu.roll(piece, (a - 1) % span_x, 1)
                    total = piece if total is None else total + piece
                bands_out.append(total.reshape(zr, 8, span_x))
            for h in range(0, bands, 2):
                grid[i, :, h * YB:h * YB + 8, :] = bands_out[h]
            grid[i, :, bands * YB:, :] = jnp.zeros((zr, yp - bands * YB, span_x), F32)
            for h in range(1, bands, 2):
                grid[i, :, h * YB:h * YB + 8, :] += bands_out[h]

    def slab(d, n):
        dy, dz = DIRS[d]
        zs = pl.ds(0, 2) if dz < 0 else pl.ds(zr - 2, 2)
        side = 0 if dy < 0 else 1
        if dy == 0:
            return grid.at[pl.ds(0, n), zs]
        if dz == 0:
            return ybuf.at[side, pl.ds(0, n)]
        return ybuf.at[side, pl.ds(0, n), zs]

    def landing(e, d, n):
        dy, dz = DIRS[d]
        if dy == 0:
            return rz.at[e, 0 if dz < 0 else 1, pl.ds(0, n)]
        if dz == 0:
            return ry.at[e, 0 if dy < 0 else 1, pl.ds(0, n)]
        return rc.at[e, (0 if dy < 0 else 2) + (0 if dz < 0 else 1), pl.ds(0, n)]

    def exchange(e, out):
        n = COMPS[e]
        ybuf[0, 0:n] = grid[0:n, :, 0:2, :]
        ybuf[1, 0:n] = grid[0:n, :, span_y:span_y + 2, :]
        order = (3, 4, 1, 6, 0, 2, 5, 7)
        for d in order:
            @pl.when(exists(d))
            def _():
                pltpu.make_async_remote_copy(
                    src_ref=slab(d, n), dst_ref=landing(e, 7 - d, n),
                    send_sem=send_sem.at[e, d], recv_sem=recv_sem.at[e, 7 - d],
                    device_id=(me_y + DIRS[d][0], me_z + DIRS[d][1]), device_id_type=MESH,
                ).start()
        for i in range(n):
            out(i)[...] = grid[i]
        for d in order:
            dy, dz = DIRS[d]

            @pl.when(exists(d))
            def _():
                copy = pltpu.make_async_remote_copy(
                    src_ref=slab(d, n), dst_ref=landing(e, d, n),
                    send_sem=send_sem.at[e, d], recv_sem=recv_sem.at[e, d],
                    device_id=(me_y + dy, me_z + dz), device_id_type=MESH,
                )
                copy.wait_recv()
                zs = slice(0, zr) if dz == 0 else (slice(0, 2) if dz < 0 else slice(zr - 2, zr))
                ys = slice(0, yp) if dy == 0 else (slice(0, 2) if dy < 0 else slice(span_y, span_y + 2))
                landed = landing(e, d, n)
                for i in range(n):
                    out(i)[zs, ys, :] += landed[i]
                copy.wait_send()

    def cell_kinds():
        shape = (zr, yp, span_x)
        gy = lax.broadcasted_iota(jnp.int32, shape, 1) - 1 + me_y * span_y
        gz = lax.broadcasted_iota(jnp.int32, shape, 0) - 1 + me_z * span_z
        sticky = (gy < 3) | (gy >= ny * span_y - 3) | (gz < 3) | (gz >= nz * span_z - 3)
        return sticky, maskx[...]

    def put_u(i, value):
        for a in range(3):
            turned = value.reshape(zr * yp, span_x)
            if a != 1:
                turned = pltpu.roll(turned, (1 - a) % span_x, 1)
            turned = turned.reshape(zr, yp, span_x)
            at = (3 * i + a) * zr * 8
            for h in range(bands):
                hi, lo = split(turned[:, h * YB:h * YB + 8, :].reshape(zr * 8, span_x))
                u_hi[at:at + zr * 8, h * span_x:(h + 1) * span_x] = hi
                u_lo[at:at + zr * 8, h * span_x:(h + 1) * span_x] = lo

    def settle(e):
        sticky, kind = cell_kinds()
        inv = 1.0 / (sums[e, 3] + MASS_REG)
        for i in range(3):
            u = sums[e, i] * inv
            if i == 1:
                u = u + DT * GRAVITY
            u = jnp.where(sticky, 0.0, u)
            for k in range(2):
                u = jnp.where(kind == float(k + 1), grip_ref[(e * 2 + k) * 3 + i], u)
            put_u(i, u)

    def settle_back(e):
        sticky, kind = cell_kinds()
        free = jnp.logical_and(jnp.logical_not(sticky), kind == 0.0)
        inv = 1.0 / (sums[e, 3] + MASS_REG)
        mass = None
        for i in range(3):
            gu = sums[2, i]
            for k in range(2):
                hit = jnp.where(kind == float(k + 1), gu, 0.0)
                part = jnp.sum(hit[1:span_z + 1], axis=0)
                part = sub_sum(part[1:span_y + 1])
                gsend[e, 3 * k + i:3 * k + i + 1, :] = part
            gs = jnp.where(free, gu * inv, 0.0)
            term = gs * sums[e, i]
            mass = term if mass is None else mass + term
            put_u(i, gs)
        put_u(3, -mass * inv)

    def gather_chunk(sl, comps):
        pz, b = geometry(sl)
        hot = oh[:, sl]
        bits = [(pz & (1 << k)) != 0 for k in range(zbits)]
        out = []
        total = 3 * comps * zr * 8
        every = jnp.dot(u_hi[0:total, :], hot, preferred_element_type=F32)
        every = every + jnp.dot(u_lo[0:total, :], hot, preferred_element_type=F32)
        for i in range(comps):
            for a in range(3):
                at = (3 * i + a) * zr * 8
                h = every[at:at + zr * 8]
                vals = [h[z * 8:(z + 1) * 8] for z in range(zr)]
                for k in reversed(range(zbits)):
                    shift = 1 << k
                    vals = [
                        jnp.where(bits[k], vals[z + shift], vals[z]) for z in range(len(vals) - shift)
                    ]
                out.append(vals)
        return out

    def moments(vals, f, b):
        wx = splines(f[0])
        wz = splines(f[2])
        wex = [wx[a] * (a - f[0]) for a in range(3)]
        wez = [wz[c] * (c - f[2]) for c in range(3)]
        wy = pick3(b, splines(f[1]))
        wey = wy * (b.astype(F32) - f[1])
        plain, first = [], []
        for i in range(3):
            x0 = [sum(wx[a] * vals[3 * i + a][c] for a in range(3)) for c in range(3)]
            x1 = [sum(wex[a] * vals[3 * i + a][c] for a in range(3)) for c in range(3)]
            z00 = sum(wz[c] * x0[c] for c in range(3))
            z10 = sum(wz[c] * x1[c] for c in range(3))
            z01 = sum(wez[c] * x0[c] for c in range(3))
            plain.append(sub_sum(wy * z00))
            first += [sub_sum(wy * z10), sub_sum(wey * z00), sub_sum(wy * z01)]
        return plain, first

    def weight_pull(vals, f, b, g, d_mat, extra):
        wx, dx = splines(f[0]), dsplines(f[0])
        wz, dz = splines(f[2]), dsplines(f[2])
        wy = pick3(b, splines(f[1]))
        dy = pick3(b, dsplines(f[1]))
        ey = b.astype(F32) - f[1]
        k_rows = [g[i] + d_mat[3 * i + 1] * ey for i in range(3)]
        by_x = [[d_mat[3 * i] * (a - f[0]) for a in range(3)] for i in range(3)]
        by_z = [[d_mat[3 * i + 2] * (c - f[2]) for c in range(3)] for i in range(3)]
        s_x = s_y = s_z = 0.0
        for c in range(3):
            q_w = q_d = 0.0
            for a in range(3):
                q = sum(vals[3 * i + a][c] * (k_rows[i] + (by_x[i][a] + by_z[i][c])) for i in range(3))
                if extra:
                    q = q + vals[9 + a][c]
                q_w = q_w + wx[a] * q
                q_d = q_d + dx[a] * q
            s_x = s_x + wz[c] * q_d
            s_y = s_y + wz[c] * q_w
            s_z = s_z + dz[c] * q_w
        return [sub_sum(wy * s_x), sub_sum(dy * s_y), sub_sum(wy * s_z)]

    states = ((off_ref, vel_ref, aff_ref, def_ref), (off1, vel1, aff1, def1))
    afters = ((off1, vel1, aff1, def1), (None, vel2, aff2, None))

    def forward(e):
        o_r, v_r, a_r, d_r = states[e]
        acc[...] = jnp.zeros_like(acc)

        @pl.loop(0, steps)
        def _(s):
            sl = pl.ds(pl.multiple_of(s * chunk, chunk), chunk)
            a_mat, _, _ = stress(row_list(a_r, sl), row_list(d_r, sl))
            scatter_chunk(s, sl, row_list(o_r, sl), row_list(v_r, sl), a_mat, live_of(s), True)

        fold(4)
        if e == 0:
            grid[4] = jnp.zeros((zr, yp, span_x), F32)
            for z in range(span_z):
                grid[4, z + 1, 1:span_y + 1, :] = mask_ref[:, z, :].astype(F32)
            barrier_wait()
        exchange(e, lambda i: sums.at[e, i] if i < 4 else maskx)
        settle(e)
        n_o, n_v, n_a, n_d = afters[e]

        @pl.loop(0, steps)
        def _(s):
            sl = pl.ds(pl.multiple_of(s * chunk, chunk), chunk)
            _, b = geometry(sl)
            f = row_list(o_r, sl)
            vals = gather_chunk(sl, 3)
            for r in range(9):
                for c in range(3):
                    node[e, 3 * r + c, :, sl] = vals[r][c]
            plain, first = moments(vals, f, b)
            new_a = [4.0 * m for m in first]
            for i in range(3):
                n_v[i:i + 1, sl] = plain[i]
            for i in range(9):
                n_a[i:i + 1, sl] = new_a[i]
            if n_o is not None:
                dm = row_list(d_r, sl)
                for i in range(3):
                    n_o[i:i + 1, sl] = f[i] + DT * plain[i]
                for i in range(3):
                    for k in range(3):
                        n_d[3 * i + k:3 * i + k + 1, sl] = dm[3 * i + k] + DT * sum(
                            new_a[3 * i + j] * dm[3 * j + k] for j in range(3)
                        )

    def gather_seeds(e, s, sl, dm):
        if e == 1:
            live = live_of(s)
            up = [[live * r for r in row_list(ref, sl)] for ref in (lo_ref, lv_ref, la_ref, ld_ref)]
        else:
            up = [row_list(ref, sl) for ref in (up_o, up_v, up_a, up_d)]
        g_o, g_v, g_a, g_d = up
        g = [g_v[i] + DT * g_o[i] for i in range(3)]
        d_mat = [
            4.0 * (g_a[3 * i + j] + DT * sum(g_d[3 * i + k] * dm[3 * j + k] for k in range(3)))
            for i in range(3)
            for j in range(3)
        ]
        return g_o, g_d, g, d_mat

    def backward(e, before, between):
        o_r, v_r, a_r, d_r = states[e]
        n_v, n_a = afters[e][1], afters[e][2]
        acc[...] = jnp.zeros_like(acc)

        @pl.loop(0, steps)
        def _(s):
            sl = pl.ds(pl.multiple_of(s * chunk, chunk), chunk)
            _, _, g, d_mat = gather_seeds(e, s, sl, row_list(d_r, sl))
            scatter_chunk(s, sl, row_list(o_r, sl), g, d_mat, None, False)

        fold(3)
        exchange(3 - e, lambda i: sums.at[2, i])
        settle_back(e)
        before()
        outs = (up_o, up_v, up_a, up_d) if e == 1 else (go_ref, gv_ref, ga_ref, gd_ref)

        def body(s):
            sl = pl.ds(pl.multiple_of(s * chunk, chunk), chunk)
            _, b = geometry(sl)
            live = live_of(s)
            f = row_list(o_r, sl)
            dm = row_list(d_r, sl)
            g_o, g_d, g, d_mat = gather_seeds(e, s, sl, dm)
            held = [[node[e, 3 * r + c, :, sl] for c in range(3)] for r in range(9)]
            pull = weight_pull(held, f, b, g, d_mat, False)
            vn = row_list(n_v, sl)
            cn = row_list(n_a, sl)
            grad_o = [
                g_o[k] + pull[k] - sum(d_mat[3 * i + k] * vn[i] for i in range(3)) for k in range(3)
            ]
            grad_d = [
                g_d[3 * j + k] + DT * sum(cn[3 * i + j] * g_d[3 * i + k] for i in range(3))
                for j in range(3)
                for k in range(3)
            ]
            vals = gather_chunk(sl, 4)
            plain, first = moments(vals, f, b)
            grad_v = [live * m for m in plain]
            grad_a = [live * m for m in first]
            a_mat, det, cof = stress(row_list(a_r, sl), dm)
            pull = weight_pull(vals, f, b, row_list(v_r, sl), a_mat, True)
            for k in range(3):
                outs[0][k:k + 1, sl] = grad_o[k] + live * pull[k] - sum(
                    a_mat[3 * i + k] * grad_v[i] for i in range(3)
                )
                outs[1][k:k + 1, sl] = grad_v[k]
            scale = (-4.0 * DT * BULK) * (grad_a[0] + grad_a[4] + grad_a[8]) / det
            for i in range(3):
                for k in range(3):
                    sym = sum((grad_a[3 * i + j] + grad_a[3 * j + i]) * dm[3 * j + k] for j in range(3))
                    at = 3 * i + k
                    outs[2][at:at + 1, sl] = grad_a[at]
                    outs[3][at:at + 1, sl] = grad_d[at] + (-4.0 * DT * SHEAR) * sym + scale * cof[at]

        pl.loop(0, steps // 2)(body)
        between()
        pl.loop(steps // 2, steps)(body)

    def grip_copy(axis, n, me, peer, slot, src, buf, ssem, rsem):
        device = (me_y, peer) if axis == "gz" else (peer, me_z)
        return pltpu.make_async_remote_copy(
            src_ref=src, dst_ref=buf.at[slot], send_sem=ssem.at[peer], recv_sem=rsem.at[slot],
            device_id=device, device_id_type=MESH,
        )

    def grip_start(axis, n, me, src, buf, ssem, rsem):
        buf[pl.ds(me, 1)] = src[...][None]

        @pl.loop(1, n)
        def _(d):
            grip_copy(axis, n, me, lax.rem(me + d, n), me, src, buf, ssem, rsem).start()

    def grip_finish(axis, n, me, src, buf, ssem, rsem):
        @pl.loop(1, n)
        def _(d):
            peer = lax.rem(me + d, n)
            copy = grip_copy(axis, n, me, peer, peer, src, buf, ssem, rsem)
            copy.wait_recv()
            copy.wait_send()

        total = buf[0]
        for at in range(1, n):
            total = total + buf[at]
        return total

    stage1 = ("gz", nz, me_z, gsend, gbuf1, gs1, gr1)
    stage2 = ("gy", ny, me_y, gsend2, gbuf2, gs2, gr2)

    def between_last():
        gsend2[...] = grip_finish(*stage1)
        grip_start(*stage2)

    def nothing():
        return None

    gsend[...] = jnp.zeros_like(gsend)
    forward(0)
    forward(1)
    backward(1, nothing, nothing)
    backward(0, lambda: grip_start(*stage1), between_last)
    total = grip_finish(*stage2)
    gg_ref[...] = jnp.broadcast_to(jnp.sum(total, axis=2, keepdims=True), total.shape)


def shards(ny, nz, offset, velocity, affine, deform, cell_index, live_count, grip_mask, grip_velocity,
           loss_offset, loss_velocity, loss_affine, loss_deform):
    span_y, span_z, span_x = grip_mask.shape
    rows = offset.shape[1]
    chunk = 1024
    zr = span_z + 2
    bands = span_y // YB
    yp = (span_y + 2 + 7) // 8 * 8
    wide = bands * span_x
    vmem = pl.BlockSpec(memory_space=pltpu.VMEM)
    smem = pl.BlockSpec(memory_space=pltpu.SMEM)
    shape = jax.ShapeDtypeStruct
    scratch = [
        pltpu.VMEM((wide, rows), BF16),
        pltpu.VMEM((rows, wide), BF16),
        pltpu.VMEM((12 * zr * 8, wide), F32),
        pltpu.VMEM((5, zr, yp, span_x), F32),
        pltpu.VMEM((2, 5, zr, 2, span_x), F32),
        pltpu.VMEM((3, 4, zr, yp, span_x), F32),
        pltpu.VMEM((zr, yp, span_x), F32),
        pltpu.VMEM((12 * zr * 8, wide), BF16),
        pltpu.VMEM((12 * zr * 8, wide), BF16),
        pltpu.VMEM((2, 27, 8, rows), F32),
        pltpu.VMEM((8, 128), F32),
        pltpu.VMEM((3, rows), F32),
        pltpu.VMEM((3, rows), F32),
        pltpu.VMEM((9, rows), F32),
        pltpu.VMEM((9, rows), F32),
        pltpu.VMEM((9, rows), F32),
        pltpu.VMEM((3, rows), F32),
        pltpu.VMEM((3, rows), F32),
        pltpu.VMEM((3, rows), F32),
        pltpu.VMEM((9, rows), F32),
        pltpu.VMEM((9, rows), F32),
        pltpu.VMEM((4, 2, 5, 2, yp, span_x), F32),
        pltpu.VMEM((4, 2, 5, zr, 2, span_x), F32),
        pltpu.VMEM((4, 4, 5, 2, 2, span_x), F32),
        pltpu.VMEM((2, 8, span_x), F32),
        pltpu.VMEM((nz, 2, 8, span_x), F32),
        pltpu.VMEM((2, 8, span_x), F32),
        pltpu.VMEM((ny, 2, 8, span_x), F32),
        pltpu.SemaphoreType.DMA((4, 8)),
        pltpu.SemaphoreType.DMA((4, 8)),
        pltpu.SemaphoreType.DMA((nz,)),
        pltpu.SemaphoreType.DMA((nz,)),
        pltpu.SemaphoreType.DMA((ny,)),
        pltpu.SemaphoreType.DMA((ny,)),
    ]
    outs = pl.pallas_call(
        functools.partial(kernel, ny, nz, span_y, span_z, span_x, rows, chunk),
        out_shape=(
            shape((3, rows), F32), shape((3, rows), F32), shape((9, rows), F32), shape((9, rows), F32),
            shape((2, 8, span_x), F32),
        ),
        in_specs=[vmem, vmem, vmem, vmem, vmem, smem, vmem, smem, vmem, vmem, vmem, vmem],
        out_specs=(vmem,) * 5,
        scratch_shapes=scratch,
        compiler_params=pltpu.CompilerParams(
            collective_id=0, has_side_effects=True, vmem_limit_bytes=56 * 1024 * 1024
        ),
    )(offset, velocity, affine, deform, cell_index.reshape(1, rows), live_count, grip_mask,
      grip_velocity.reshape(-1), loss_offset, loss_velocity, loss_affine, loss_deform)
    grad_grip = outs[4][:, :6, 0].reshape(2, 2, 3)
    return (outs[0], outs[1], outs[2], outs[3], grad_grip)


def solution(mesh):
    rows = P(None, ("gy", "gz"))
    ny, nz = mesh.shape["gy"], mesh.shape["gz"]
    return jax.shard_map(
        functools.partial(shards, ny, nz),
        mesh=mesh,
        in_specs=(
            rows, rows, rows, rows, P(("gy", "gz")), P(("gy", "gz")), P("gy", "gz", None), P(),
            rows, rows, rows, rows,
        ),
        out_specs=(rows, rows, rows, rows, P()),
        check_vma=False,
    )
```

```python
import functools

import jax
import jax.numpy as jnp
from jax import lax
from jax.experimental import pallas as pl
from jax.experimental.pallas import tpu as pltpu
from jax.sharding import PartitionSpec as P

DT = 0.05
SHEAR = 10.0
BULK = 10.0
GRAVITY = -2.0
MASS_REG = 0.1
F32 = jnp.float32
BF16 = jnp.bfloat16
MESH = pl.DeviceIdType.MESH
DIRS = [(-1, -1), (-1, 0), (-1, 1), (0, -1), (0, 1), (1, -1), (1, 0), (1, 1)]
YB = 4
COMPS = (5, 4, 3, 3)


def splines(f):
    return (0.5 * (1.5 - f) ** 2, 0.75 - (f - 1.0) ** 2, 0.5 * (f - 0.5) ** 2)


def dsplines(f):
    return (f - 1.5, -2.0 * (f - 1.0), f - 0.5)


def pick3(b, vals):
    return jnp.where(b == 0, vals[0], jnp.where(b == 1, vals[1], jnp.where(b == 2, vals[2], 0.0)))


def sub_sum(x):
    return jnp.sum(x, axis=0, keepdims=True)


def split(x):
    hi = x.astype(BF16)
    lo = (x - hi.astype(F32)).astype(BF16)
    return hi, lo


def stress(c_rows, f_rows):
    f = f_rows
    cof = [
        f[4] * f[8] - f[5] * f[7],
        f[5] * f[6] - f[3] * f[8],
        f[3] * f[7] - f[4] * f[6],
        f[2] * f[7] - f[1] * f[8],
        f[0] * f[8] - f[2] * f[6],
        f[1] * f[6] - f[0] * f[7],
        f[1] * f[5] - f[2] * f[4],
        f[2] * f[3] - f[0] * f[5],
        f[0] * f[4] - f[1] * f[3],
    ]
    det = f[0] * cof[0] + f[1] * cof[1] + f[2] * cof[2]
    log_det = jnp.log(det)
    a_rows = []
    for i in range(3):
        for j in range(3):
            left = f[3 * i] * f[3 * j] + f[3 * i + 1] * f[3 * j + 1] + f[3 * i + 2] * f[3 * j + 2]
            tau = SHEAR * (left - 1.0) + BULK * log_det if i == j else SHEAR * left
            a_rows.append(c_rows[3 * i + j] - 4.0 * DT * tau)
    return a_rows, det, cof


def kernel(
    ny, nz, span_y, span_z, span_x, rows, chunk,
    off_ref, vel_ref, aff_ref, def_ref, idx_ref, live_ref, mask_ref, grip_ref,
    lo_ref, lv_ref, la_ref, ld_ref,
    go_ref, gv_ref, ga_ref, gd_ref, gg_ref,
    oh, oht, acc, grid, ybuf, sums, maskx, u_hi, u_lo, node, node_b,
    off1, vel1, aff1, def1, aff2, vel2, up_o, up_v, up_a, up_d,
    rz, ry, rc, gsend, gbuf1, gsend2, gbuf2,
    send_sem, recv_sem, gs1, gr1, gs2, gr2,
):
    me_y = lax.axis_index("gy")
    me_z = lax.axis_index("gz")
    zr = span_z + 2
    bands = span_y // YB
    yp = grid.shape[2]
    zbits = span_z.bit_length() - 1
    xbits = span_x.bit_length() - 1
    steps = rows // chunk

    barrier = pltpu.get_barrier_semaphore()

    @pl.loop(1, nz)
    def _(d):
        pl.semaphore_signal(barrier, inc=1, device_id=(me_y, lax.rem(me_z + d, nz)), device_id_type=MESH)

    @pl.loop(1, ny)
    def _(d):
        pl.semaphore_signal(barrier, inc=1, device_id=(lax.rem(me_y + d, ny), me_z), device_id_type=MESH)

    def exists(d):
        dy, dz = DIRS[d]
        ok = None
        if dy:
            ok = me_y > 0 if dy < 0 else me_y < ny - 1
        if dz:
            okz = me_z > 0 if dz < 0 else me_z < nz - 1
            ok = okz if ok is None else jnp.logical_and(ok, okz)
        return ok

    for d in (0, 2, 5, 7):
        @pl.when(exists(d))
        def _():
            pl.semaphore_signal(
                barrier, inc=1, device_id=(me_y + DIRS[d][0], me_z + DIRS[d][1]), device_id_type=MESH
            )

    def barrier_wait():
        sides_y = (me_y > 0).astype(jnp.int32) + (me_y < ny - 1).astype(jnp.int32)
        sides_z = (me_z > 0).astype(jnp.int32) + (me_z < nz - 1).astype(jnp.int32)
        pl.semaphore_wait(barrier, ny + nz - 2 + sides_y * sides_z)

    def column(sl):
        idx = idx_ref[:, sl]
        rem = idx >> xbits
        return ((rem >> (zbits + 2)) << xbits) + (idx & (span_x - 1))

    @pl.loop(0, steps)
    def _(s):
        sl = pl.ds(pl.multiple_of(s * chunk, chunk), chunk)
        col = column(sl)
        wide = bands * span_x
        col_t = jnp.transpose(jnp.broadcast_to(col.astype(F32), (128, chunk)))
        lane = lax.broadcasted_iota(jnp.int32, (chunk, 128), 1)
        for part in range(wide // 128):
            oht[sl, part * 128:(part + 1) * 128] = jnp.where(
                col_t == (lane + part * 128).astype(F32), 1.0, 0.0
            ).astype(BF16)

    def build_oh():
        @pl.loop(0, steps)
        def _(s):
            sl = pl.ds(pl.multiple_of(s * chunk, chunk), chunk)
            rows_iota = lax.broadcasted_iota(jnp.int32, (bands * span_x, chunk), 0)
            oh[:, sl] = jnp.where(rows_iota == column(sl), 1.0, 0.0).astype(BF16)

    def geometry(sl):
        rem = idx_ref[:, sl] >> xbits
        pz = rem & (span_z - 1)
        yl = (rem >> zbits) & (YB - 1)
        b = lax.broadcasted_iota(jnp.int32, (8, chunk), 0) - yl
        return pz, b

    def live_of(s):
        lane = lax.broadcasted_iota(jnp.int32, (1, chunk), 1) + s * chunk
        return jnp.where(lane < live_ref[0], 1.0, 0.0)

    def row_list(ref, sl):
        return [ref[i:i + 1, sl] for i in range(ref.shape[0])]

    def scatter_chunk(s, sl, f, v, a_mat, scale, mass):
        pz, b = geometry(sl)
        wx = splines(f[0])
        ex = [k - f[0] for k in range(3)]
        wy = pick3(b, splines(f[1]))
        if scale is not None:
            wy = wy * scale
        ey = b.astype(F32) - f[1]
        sz = splines(f[2])
        c = [z - pz for z in range(zr)]
        wyz = [wy * pick3(c[z], sz) for z in range(zr)]
        ez = [c[z].astype(F32) - f[2] for z in range(zr)]
        his, los = [], []
        for i in range(3):
            vy = v[i] + a_mat[3 * i + 1] * ey
            t = [wyz[z] * (vy + a_mat[3 * i + 2] * ez[z]) for z in range(zr)]
            for a in range(3):
                coef = wx[a] * (a_mat[3 * i] * ex[a])
                block = jnp.concatenate([t[z] * wx[a] + wyz[z] * coef for z in range(zr)], axis=0)
                hi, lo = split(block)
                his.append(hi)
                los.append(lo)
        if mass:
            for a in range(3):
                block = jnp.concatenate([wyz[z] * wx[a] for z in range(zr)], axis=0)
                hi, lo = split(block)
                his.append(hi)
                los.append(lo)
        hot = oht[sl, :]
        total = (12 if mass else 9) * zr * 8
        part = jnp.dot(jnp.concatenate(his, axis=0), hot, preferred_element_type=F32)
        part = part + jnp.dot(jnp.concatenate(los, axis=0), hot, preferred_element_type=F32)
        acc[0:total, :] += part

    def fold(comps):
        for i in range(comps):
            bands_out = []
            for h in range(bands):
                total = None
                for a in range(3):
                    at = (3 * i + a) * zr * 8
                    piece = acc[at:at + zr * 8, h * span_x:(h + 1) * span_x]
                    if a != 1:
                        piece = pltpu.roll(piece, (a - 1) % span_x, 1)
                    total = piece if total is None else total + piece
                bands_out.append(total.reshape(zr, 8, span_x))
            for h in range(0, bands, 2):
                grid[i, :, h * YB:h * YB + 8, :] = bands_out[h]
            grid[i, :, bands * YB:, :] = jnp.zeros((zr, yp - bands * YB, span_x), F32)
            for h in range(1, bands, 2):
                grid[i, :, h * YB:h * YB + 8, :] += bands_out[h]

    def slab(d, n):
        dy, dz = DIRS[d]
        zs = pl.ds(0, 2) if dz < 0 else pl.ds(zr - 2, 2)
        side = 0 if dy < 0 else 1
        if dy == 0:
            return grid.at[pl.ds(0, n), zs]
        if dz == 0:
            return ybuf.at[side, pl.ds(0, n)]
        return ybuf.at[side, pl.ds(0, n), zs]

    def landing(e, d, n):
        dy, dz = DIRS[d]
        if dy == 0:
            return rz.at[e, 0 if dz < 0 else 1, pl.ds(0, n)]
        if dz == 0:
            return ry.at[e, 0 if dy < 0 else 1, pl.ds(0, n)]
        return rc.at[e, (0 if dy < 0 else 2) + (0 if dz < 0 else 1), pl.ds(0, n)]

    def exchange(e, out, during):
        n = COMPS[e]
        ybuf[0, 0:n] = grid[0:n, :, 0:2, :]
        ybuf[1, 0:n] = grid[0:n, :, span_y:span_y + 2, :]
        order = (3, 4, 1, 6, 0, 2, 5, 7)
        for d in order:
            @pl.when(exists(d))
            def _():
                pltpu.make_async_remote_copy(
                    src_ref=slab(d, n), dst_ref=landing(e, 7 - d, n),
                    send_sem=send_sem.at[e, d], recv_sem=recv_sem.at[e, 7 - d],
                    device_id=(me_y + DIRS[d][0], me_z + DIRS[d][1]), device_id_type=MESH,
                ).start()
        for i in range(n):
            out(i)[...] = grid[i]
        during()
        for d in order:
            dy, dz = DIRS[d]

            @pl.when(exists(d))
            def _():
                copy = pltpu.make_async_remote_copy(
                    src_ref=slab(d, n), dst_ref=landing(e, d, n),
                    send_sem=send_sem.at[e, d], recv_sem=recv_sem.at[e, d],
                    device_id=(me_y + dy, me_z + dz), device_id_type=MESH,
                )
                copy.wait_recv()
                zs = slice(0, zr) if dz == 0 else (slice(0, 2) if dz < 0 else slice(zr - 2, zr))
                ys = slice(0, yp) if dy == 0 else (slice(0, 2) if dy < 0 else slice(span_y, span_y + 2))
                landed = landing(e, d, n)
                for i in range(n):
                    out(i)[zs, ys, :] += landed[i]
                copy.wait_send()

    def cell_kinds():
        shape = (zr, yp, span_x)
        gy = lax.broadcasted_iota(jnp.int32, shape, 1) - 1 + me_y * span_y
        gz = lax.broadcasted_iota(jnp.int32, shape, 0) - 1 + me_z * span_z
        sticky = (gy < 3) | (gy >= ny * span_y - 3) | (gz < 3) | (gz >= nz * span_z - 3)
        return sticky, maskx[...]

    def put_u(i, value):
        for a in range(3):
            turned = value.reshape(zr * yp, span_x)
            if a != 1:
                turned = pltpu.roll(turned, (1 - a) % span_x, 1)
            turned = turned.reshape(zr, yp, span_x)
            at = (3 * i + a) * zr * 8
            for h in range(bands):
                hi, lo = split(turned[:, h * YB:h * YB + 8, :].reshape(zr * 8, span_x))
                u_hi[at:at + zr * 8, h * span_x:(h + 1) * span_x] = hi
                u_lo[at:at + zr * 8, h * span_x:(h + 1) * span_x] = lo

    def settle(e):
        sticky, kind = cell_kinds()
        inv = 1.0 / (sums[e, 3] + MASS_REG)
        for i in range(3):
            u = sums[e, i] * inv
            if i == 1:
                u = u + DT * GRAVITY
            u = jnp.where(sticky, 0.0, u)
            for k in range(2):
                u = jnp.where(kind == float(k + 1), grip_ref[(e * 2 + k) * 3 + i], u)
            put_u(i, u)

    def settle_back(e):
        sticky, kind = cell_kinds()
        free = jnp.logical_and(jnp.logical_not(sticky), kind == 0.0)
        inv = 1.0 / (sums[e, 3] + MASS_REG)
        mass = None
        for i in range(3):
            gu = sums[2, i]
            for k in range(2):
                hit = jnp.where(kind == float(k + 1), gu, 0.0)
                part = jnp.sum(hit[1:span_z + 1], axis=0)
                part = sub_sum(part[1:span_y + 1])
                gsend[e, 3 * k + i:3 * k + i + 1, :] = part
            gs = jnp.where(free, gu * inv, 0.0)
            term = gs * sums[e, i]
            mass = term if mass is None else mass + term
            put_u(i, gs)
        put_u(3, -mass * inv)

    def gather_chunk(sl, comps):
        pz, b = geometry(sl)
        hot = oh[:, sl]
        bits = [(pz & (1 << k)) != 0 for k in range(zbits)]
        out = []
        total = 3 * comps * zr * 8
        every = jnp.dot(u_hi[0:total, :], hot, preferred_element_type=F32)
        every = every + jnp.dot(u_lo[0:total, :], hot, preferred_element_type=F32)
        for i in range(comps):
            for a in range(3):
                at = (3 * i + a) * zr * 8
                h = every[at:at + zr * 8]
                vals = [h[z * 8:(z + 1) * 8] for z in range(zr)]
                for k in reversed(range(zbits)):
                    shift = 1 << k
                    vals = [
                        jnp.where(bits[k], vals[z + shift], vals[z]) for z in range(len(vals) - shift)
                    ]
                out.append(vals)
        return out

    def moments(vals, f, b):
        wx = splines(f[0])
        wz = splines(f[2])
        wex = [wx[a] * (a - f[0]) for a in range(3)]
        wez = [wz[c] * (c - f[2]) for c in range(3)]
        wy = pick3(b, splines(f[1]))
        wey = wy * (b.astype(F32) - f[1])
        plain, first = [], []
        for i in range(3):
            x0 = [sum(wx[a] * vals[3 * i + a][c] for a in range(3)) for c in range(3)]
            x1 = [sum(wex[a] * vals[3 * i + a][c] for a in range(3)) for c in range(3)]
            z00 = sum(wz[c] * x0[c] for c in range(3))
            z10 = sum(wz[c] * x1[c] for c in range(3))
            z01 = sum(wez[c] * x0[c] for c in range(3))
            plain.append(sub_sum(wy * z00))
            first += [sub_sum(wy * z10), sub_sum(wey * z00), sub_sum(wy * z01)]
        return plain, first

    def weight_pull(vals, f, b, g, d_mat, extra):
        wx, dx = splines(f[0]), dsplines(f[0])
        wz, dz = splines(f[2]), dsplines(f[2])
        wy = pick3(b, splines(f[1]))
        dy = pick3(b, dsplines(f[1]))
        ey = b.astype(F32) - f[1]
        k_rows = [g[i] + d_mat[3 * i + 1] * ey for i in range(3)]
        by_x = [[d_mat[3 * i] * (a - f[0]) for a in range(3)] for i in range(3)]
        by_z = [[d_mat[3 * i + 2] * (c - f[2]) for c in range(3)] for i in range(3)]
        s_x = s_y = s_z = 0.0
        for c in range(3):
            q_w = q_d = 0.0
            for a in range(3):
                q = sum(vals[3 * i + a][c] * (k_rows[i] + (by_x[i][a] + by_z[i][c])) for i in range(3))
                if extra:
                    q = q + vals[9 + a][c]
                q_w = q_w + wx[a] * q
                q_d = q_d + dx[a] * q
            s_x = s_x + wz[c] * q_d
            s_y = s_y + wz[c] * q_w
            s_z = s_z + dz[c] * q_w
        return [sub_sum(wy * s_x), sub_sum(dy * s_y), sub_sum(wy * s_z)]

    states = ((off_ref, vel_ref, aff_ref, def_ref), (off1, vel1, aff1, def1))
    afters = ((off1, vel1, aff1, def1), (None, vel2, aff2, None))

    def forward(e):
        o_r, v_r, a_r, d_r = states[e]
        acc[...] = jnp.zeros_like(acc)

        @pl.loop(0, steps)
        def _(s):
            sl = pl.ds(pl.multiple_of(s * chunk, chunk), chunk)
            a_mat, _, _ = stress(row_list(a_r, sl), row_list(d_r, sl))
            scatter_chunk(s, sl, row_list(o_r, sl), row_list(v_r, sl), a_mat, live_of(s), True)

        fold(4)
        if e == 0:
            grid[4] = jnp.zeros((zr, yp, span_x), F32)
            for z in range(span_z):
                grid[4, z + 1, 1:span_y + 1, :] = mask_ref[:, z, :].astype(F32)
            barrier_wait()
        exchange(e, lambda i: sums.at[e, i] if i < 4 else maskx, build_oh if e == 0 else nothing)
        settle(e)
        n_o, n_v, n_a, n_d = afters[e]

        @pl.loop(0, steps)
        def _(s):
            sl = pl.ds(pl.multiple_of(s * chunk, chunk), chunk)
            _, b = geometry(sl)
            f = row_list(o_r, sl)
            vals = gather_chunk(sl, 3)
            for r in range(9):
                for c in range(3):
                    node[e, 3 * r + c, :, sl] = vals[r][c]
            plain, first = moments(vals, f, b)
            new_a = [4.0 * m for m in first]
            for i in range(3):
                n_v[i:i + 1, sl] = plain[i]
            for i in range(9):
                n_a[i:i + 1, sl] = new_a[i]
            if n_o is not None:
                dm = row_list(d_r, sl)
                for i in range(3):
                    n_o[i:i + 1, sl] = f[i] + DT * plain[i]
                for i in range(3):
                    for k in range(3):
                        n_d[3 * i + k:3 * i + k + 1, sl] = dm[3 * i + k] + DT * sum(
                            new_a[3 * i + j] * dm[3 * j + k] for j in range(3)
                        )

    def gather_seeds(e, s, sl, dm):
        if e == 1:
            live = live_of(s)
            up = [[live * r for r in row_list(ref, sl)] for ref in (lo_ref, lv_ref, la_ref, ld_ref)]
        else:
            up = [row_list(ref, sl) for ref in (up_o, up_v, up_a, up_d)]
        g_o, g_v, g_a, g_d = up
        g = [g_v[i] + DT * g_o[i] for i in range(3)]
        d_mat = [
            4.0 * (g_a[3 * i + j] + DT * sum(g_d[3 * i + k] * dm[3 * j + k] for k in range(3)))
            for i in range(3)
            for j in range(3)
        ]
        return g_o, g_d, g, d_mat

    def backward(e, before, between):
        o_r, v_r, a_r, d_r = states[e]
        n_v, n_a = afters[e][1], afters[e][2]
        acc[...] = jnp.zeros_like(acc)

        @pl.loop(0, steps)
        def _(s):
            sl = pl.ds(pl.multiple_of(s * chunk, chunk), chunk)
            _, _, g, d_mat = gather_seeds(e, s, sl, row_list(d_r, sl))
            scatter_chunk(s, sl, row_list(o_r, sl), g, d_mat, None, False)

        fold(3)
        outs = (up_o, up_v, up_a, up_d) if e == 1 else (go_ref, gv_ref, ga_ref, gd_ref)

        def through_gather(s):
            sl = pl.ds(pl.multiple_of(s * chunk, chunk), chunk)
            _, b = geometry(sl)
            f = row_list(o_r, sl)
            g_o, g_d, g, d_mat = gather_seeds(e, s, sl, row_list(d_r, sl))
            held = [[node[e, 3 * r + c, :, sl] for c in range(3)] for r in range(9)]
            pull = weight_pull(held, f, b, g, d_mat, False)
            vn = row_list(n_v, sl)
            cn = row_list(n_a, sl)
            grad_o = [
                g_o[k] + pull[k] - sum(d_mat[3 * i + k] * vn[i] for i in range(3)) for k in range(3)
            ]
            grad_d = [
                g_d[3 * j + k] + DT * sum(cn[3 * i + j] * g_d[3 * i + k] for i in range(3))
                for j in range(3)
                for k in range(3)
            ]
            for k in range(3):
                outs[0][k:k + 1, sl] = grad_o[k]
            for k in range(9):
                outs[3][k:k + 1, sl] = grad_d[k]

        exchange(3 - e, lambda i: sums.at[2, i], lambda: pl.loop(0, steps)(through_gather))
        settle_back(e)
        before()

        def body(s):
            sl = pl.ds(pl.multiple_of(s * chunk, chunk), chunk)
            _, b = geometry(sl)
            live = live_of(s)
            f = row_list(o_r, sl)
            dm = row_list(d_r, sl)
            grad_o = row_list(outs[0], sl)
            grad_d = row_list(outs[3], sl)
            vals = gather_chunk(sl, 4)
            plain, first = moments(vals, f, b)
            grad_v = [live * m for m in plain]
            grad_a = [live * m for m in first]
            a_mat, det, cof = stress(row_list(a_r, sl), dm)
            pull = weight_pull(vals, f, b, row_list(v_r, sl), a_mat, True)
            for k in range(3):
                outs[0][k:k + 1, sl] = grad_o[k] + live * pull[k] - sum(
                    a_mat[3 * i + k] * grad_v[i] for i in range(3)
                )
                outs[1][k:k + 1, sl] = grad_v[k]
            scale = (-4.0 * DT * BULK) * (grad_a[0] + grad_a[4] + grad_a[8]) / det
            for i in range(3):
                for k in range(3):
                    sym = sum((grad_a[3 * i + j] + grad_a[3 * j + i]) * dm[3 * j + k] for j in range(3))
                    at = 3 * i + k
                    outs[2][at:at + 1, sl] = grad_a[at]
                    outs[3][at:at + 1, sl] = grad_d[at] + (-4.0 * DT * SHEAR) * sym + scale * cof[at]

        pl.loop(0, steps // 2)(body)
        between()
        pl.loop(steps // 2, steps)(body)

    def grip_copy(axis, n, me, peer, slot, src, buf, ssem, rsem):
        device = (me_y, peer) if axis == "gz" else (peer, me_z)
        return pltpu.make_async_remote_copy(
            src_ref=src, dst_ref=buf.at[slot], send_sem=ssem.at[peer], recv_sem=rsem.at[slot],
            device_id=device, device_id_type=MESH,
        )

    def grip_start(axis, n, me, src, buf, ssem, rsem):
        buf[pl.ds(me, 1)] = src[...][None]

        @pl.loop(1, n)
        def _(d):
            grip_copy(axis, n, me, lax.rem(me + d, n), me, src, buf, ssem, rsem).start()

    def grip_finish(axis, n, me, src, buf, ssem, rsem):
        @pl.loop(1, n)
        def _(d):
            peer = lax.rem(me + d, n)
            copy = grip_copy(axis, n, me, peer, peer, src, buf, ssem, rsem)
            copy.wait_recv()
            copy.wait_send()

        total = buf[0]
        for at in range(1, n):
            total = total + buf[at]
        return total

    stage1 = ("gz", nz, me_z, gsend, gbuf1, gs1, gr1)
    stage2 = ("gy", ny, me_y, gsend2, gbuf2, gs2, gr2)

    def between_last():
        gsend2[...] = grip_finish(*stage1)
        grip_start(*stage2)

    def nothing():
        return None

    gsend[...] = jnp.zeros_like(gsend)
    forward(0)
    forward(1)
    backward(1, nothing, nothing)
    backward(0, lambda: grip_start(*stage1), between_last)
    total = grip_finish(*stage2)
    gg_ref[...] = jnp.broadcast_to(jnp.sum(total, axis=2, keepdims=True), total.shape)


def shards(ny, nz, offset, velocity, affine, deform, cell_index, live_count, grip_mask, grip_velocity,
           loss_offset, loss_velocity, loss_affine, loss_deform):
    span_y, span_z, span_x = grip_mask.shape
    rows = offset.shape[1]
    chunk = 1024
    zr = span_z + 2
    bands = span_y // YB
    yp = (span_y + 2 + 7) // 8 * 8
    wide = bands * span_x
    vmem = pl.BlockSpec(memory_space=pltpu.VMEM)
    smem = pl.BlockSpec(memory_space=pltpu.SMEM)
    shape = jax.ShapeDtypeStruct
    scratch = [
        pltpu.VMEM((wide, rows), BF16),
        pltpu.VMEM((rows, wide), BF16),
        pltpu.VMEM((12 * zr * 8, wide), F32),
        pltpu.VMEM((5, zr, yp, span_x), F32),
        pltpu.VMEM((2, 5, zr, 2, span_x), F32),
        pltpu.VMEM((3, 4, zr, yp, span_x), F32),
        pltpu.VMEM((zr, yp, span_x), F32),
        pltpu.VMEM((12 * zr * 8, wide), BF16),
        pltpu.VMEM((12 * zr * 8, wide), BF16),
        pltpu.VMEM((2, 27, 8, rows), F32),
        pltpu.VMEM((8, 128), F32),
        pltpu.VMEM((3, rows), F32),
        pltpu.VMEM((3, rows), F32),
        pltpu.VMEM((9, rows), F32),
        pltpu.VMEM((9, rows), F32),
        pltpu.VMEM((9, rows), F32),
        pltpu.VMEM((3, rows), F32),
        pltpu.VMEM((3, rows), F32),
        pltpu.VMEM((3, rows), F32),
        pltpu.VMEM((9, rows), F32),
        pltpu.VMEM((9, rows), F32),
        pltpu.VMEM((4, 2, 5, 2, yp, span_x), F32),
        pltpu.VMEM((4, 2, 5, zr, 2, span_x), F32),
        pltpu.VMEM((4, 4, 5, 2, 2, span_x), F32),
        pltpu.VMEM((2, 8, span_x), F32),
        pltpu.VMEM((nz, 2, 8, span_x), F32),
        pltpu.VMEM((2, 8, span_x), F32),
        pltpu.VMEM((ny, 2, 8, span_x), F32),
        pltpu.SemaphoreType.DMA((4, 8)),
        pltpu.SemaphoreType.DMA((4, 8)),
        pltpu.SemaphoreType.DMA((nz,)),
        pltpu.SemaphoreType.DMA((nz,)),
        pltpu.SemaphoreType.DMA((ny,)),
        pltpu.SemaphoreType.DMA((ny,)),
    ]
    outs = pl.pallas_call(
        functools.partial(kernel, ny, nz, span_y, span_z, span_x, rows, chunk),
        out_shape=(
            shape((3, rows), F32), shape((3, rows), F32), shape((9, rows), F32), shape((9, rows), F32),
            shape((2, 8, span_x), F32),
        ),
        in_specs=[vmem, vmem, vmem, vmem, vmem, smem, vmem, smem, vmem, vmem, vmem, vmem],
        out_specs=(vmem,) * 5,
        scratch_shapes=scratch,
        compiler_params=pltpu.CompilerParams(
            collective_id=0, has_side_effects=True, vmem_limit_bytes=56 * 1024 * 1024
        ),
    )(offset, velocity, affine, deform, cell_index.reshape(1, rows), live_count, grip_mask,
      grip_velocity.reshape(-1), loss_offset, loss_velocity, loss_affine, loss_deform)
    grad_grip = outs[4][:, :6, 0].reshape(2, 2, 3)
    return (outs[0], outs[1], outs[2], outs[3], grad_grip)


def solution(mesh):
    rows = P(None, ("gy", "gz"))
    ny, nz = mesh.shape["gy"], mesh.shape["gz"]
    return jax.shard_map(
        functools.partial(shards, ny, nz),
        mesh=mesh,
        in_specs=(
            rows, rows, rows, rows, P(("gy", "gz")), P(("gy", "gz")), P("gy", "gz", None), P(),
            rows, rows, rows, rows,
        ),
        out_specs=(rows, rows, rows, rows, P()),
        check_vma=False,
    )
```
